256 devices in a mesh: ctx: 32 (over x, z_hi, core), chan: 8 (over y, z_lo).
Axes of the slice: x: 4, y: 4, z: 8 (z_hi: 4, z_lo: 2; z = z_hi * 2 + z_lo), core: 2. Of those that a mesh axis runs over, the one named last changes fastest.
Arguments:
- query_proj: bfloat16 [16384, 4096], P('ctx', 'chan'), may hold values from -6 to 6
- key_proj: bfloat16 [16384, 4096], P('ctx', 'chan'), may hold values from -6 to 6
- value_proj: bfloat16 [16384, 4096], P('ctx', 'chan'), may hold values from -6 to 6
- long_filter: float32 [16384, 4096], P('ctx', 'chan'), may hold values from 0 to 1
- skip_gain: float32 [4096], P('chan'), may hold values from 0.5 to 1.5
- out_weight: bfloat16 [4096, 4096], P('ctx', 'chan'), may hold values from -0.09375 to 0.09375
Outputs:
- mixed: bfloat16 [16384, 4096], P('ctx', 'chan')
The draws below stay inside these ranges and needn't reach their ends.
All inputs are finite; a program needn't handle non-finite values.
Results may differ from the reference program's by a relative error of at most 0.0049.
Values may be sent and summed in bfloat16 or wider, within the bound.
No kernel may reach another device: no remote copies, remote signals or barrier semaphores. Data moves between devices by JAX's collectives and lax.ppermute only.
A program may use at most 128 MiB of HBM per device.

```python
import math
import jax
import jax.numpy as jnp
from jax import lax

D = 4096
TOKENS = 16384


def draw_long_filter(key, part):
    key = jax.random.fold_in(key, 11)
    key_slow, key_fast, key_pick, key_rough, key_share = jax.random.split(key, 5)
    slow_rate = jnp.exp(jax.random.uniform(key_slow, (D,), jnp.float32, jnp.log(0.3 / TOKENS), jnp.log(2.0 / TOKENS)))
    fast_rate = jnp.exp(jax.random.uniform(key_fast, (D,), jnp.float32, jnp.log(1.0 / 50.0), jnp.log(1.0 / 25.0)))
    share_slow = 0.5
    rough = 1.0 + 0.6 * jax.random.uniform(key_rough, (TOKENS, D), jnp.float32, -1.0, 1.0)
    picked = jax.random.bernoulli(key_pick, share_slow, (D,))
    level = jax.random.uniform(key_share, (D,), jnp.float32, 0.0, 1.0)
    kept = jnp.where(picked, jnp.exp(jnp.log(0.2) + level * jnp.log(4.0)), jnp.exp(jnp.log(0.01) + level * jnp.log(10.0)))
    slow_amp = jnp.sqrt(kept * (1.0 - jnp.exp(-2.0 * slow_rate)))
    fast_amp = jnp.sqrt((1.0 - kept) * (1.0 - jnp.exp(-2.0 * fast_rate)))
    lags = jnp.arange(TOKENS, dtype=jnp.float32)[:, None]
    shape_value = fast_amp[None, :] * jnp.exp(-fast_rate[None, :] * lags) + slow_amp[None, :] * jnp.exp(-slow_rate[None, :] * lags)
    return (shape_value * rough).astype(jnp.float32)


def shard_levels(rng, dims, cuts, least, top_value):
    level, own = 1.0, jax.random.fold_in(rng, 6)
    for dim, shards_of in cuts:
        draws = jnp.exp(jax.random.uniform(jax.random.fold_in(own, dim), (shards_of,), jnp.float32, least / len(cuts), top_value / len(cuts)))
        level = level * jnp.repeat(draws, dims[dim] // shards_of).reshape([-1 if axis == dim else 1 for axis in range(len(dims))])
    return level


def scatter_about(rng, dims, spread, most, shards=(), held_as=jnp.bfloat16):
    values = spread * jax.random.normal(rng, dims, jnp.float32)
    if shards:
        values = values * shard_levels(rng, dims, shards, -0.22, 0.18)
    return jnp.clip(values, -most, most).astype(held_as)


def setup_inputs(seed: int = 0) -> dict:
    seeds = jax.random.split(jax.random.key(seed), 7)
    query_proj = scatter_about(seeds[0], (TOKENS, D), 1.0, 6.0, ((0, 32), (1, 8)))
    key_proj = scatter_about(seeds[1], (TOKENS, D), 1.0, 6.0, ((0, 32), (1, 8)))
    value_proj = scatter_about(seeds[2], (TOKENS, D), 1.0, 6.0, ((0, 32), (1, 8)))
    long_filter = draw_long_filter(jax.random.fold_in(seeds[6], 71), 0)
    skip_gain = jnp.clip(0.5 + 1.0 * jax.random.uniform(seeds[4], (D,), jnp.float32) ** shard_levels(seeds[4], (D,), ((0, 8),), -0.2, 0.2), 0.5, 1.5)
    out_weight = scatter_about(seeds[5], (D, D), D ** -0.5, 0.09375, ((0, 32), (1, 8)))
    return dict(query_proj=query_proj, key_proj=key_proj, value_proj=value_proj, long_filter=long_filter, skip_gain=skip_gain, out_weight=out_weight)


def reference(query_proj, key_proj, value_proj, long_filter, skip_gain, out_weight):
    source = key_proj.astype(jnp.float32) * value_proj.astype(jnp.float32)
    block_width = math.gcd(D, 512)
    block_count = D // block_width

    def convolve(pair):
        signal, kernel = pair
        length = 2 * TOKENS
        spectrum = jnp.fft.rfft(signal, n=length, axis=0) * jnp.fft.rfft(kernel, n=length, axis=0)
        return jnp.fft.irfft(spectrum, n=length, axis=0)[:TOKENS]

    stacked_source = source.reshape(TOKENS, block_count, block_width).transpose(1, 0, 2)
    stacked_filter = long_filter.reshape(TOKENS, block_count, block_width).transpose(1, 0, 2)
    conv = lax.map(convolve, (stacked_source, stacked_filter))
    conv = conv.transpose(1, 0, 2).reshape(TOKENS, D)
    gated = (query_proj.astype(jnp.float32) * (conv + skip_gain[None, :] * source)).astype(jnp.bfloat16)
    return jnp.dot(gated, out_weight, preferred_element_type=jnp.float32).astype(jnp.bfloat16)
```

```python
import functools
import math

import jax
import jax.numpy as jnp
import numpy as np
from jax import lax
from jax.experimental import pallas as pl
from jax.experimental.pallas import tpu as pltpu
from jax.sharding import Mesh
from jax.sharding import PartitionSpec as P

AXES = ("x", "zh", "core", "y", "zl")
LINE = ("x", "zh", "zl")
BLOCKS = 32
BLOCK = 512
SLICE = 8
HALF = 256
STEPS = 64
INNER = 256
PERIOD = 32768
VMEM = 56 * 1024 * 1024
SWAP = [(0, 0), (1, 2), (2, 1), (3, 3)]
PAIR = [(0, 1), (1, 0)]


def halves(table):
    high = table.astype(np.float32).astype(jnp.bfloat16)
    low = (table - high.astype(np.float64)).astype(np.float32).astype(jnp.bfloat16)
    return high, low


def tables():
    odd = np.arange(STEPS) + 0.5
    steps = np.arange(STEPS)
    inner = np.arange(INNER)
    outer = 2 * math.pi * np.outer(odd, steps) / (2 * STEPS)
    same = np.eye(SLICE)
    order = steps.reshape(BLOCKS, 2).T.reshape(-1)
    cos_o, sin_o = np.cos(outer)[:, order], np.sin(outer)[:, order]
    first = np.concatenate([np.kron(cos_o, same), np.kron(-sin_o, same)], 0)
    last = np.concatenate([np.kron(cos_o.T, same), np.kron(-sin_o.T, same)], 1) / (PERIOD // 2)
    turn = 2 * math.pi * np.outer(odd, inner) / PERIOD
    turn = np.stack([np.cos(turn), np.sin(turn)]).astype(np.float32)
    angle = 2 * math.pi * (np.outer(inner, inner) % INNER) / INNER
    cos_i, sin_i = np.cos(angle), np.sin(angle)
    ahead = np.block([[cos_i, -sin_i], [sin_i, cos_i]])
    back = np.block([[cos_i, sin_i], [-sin_i, cos_i]])
    first_high, first_low = halves(first)
    last_high, last_low = halves(last)
    ahead_high, ahead_low = halves(ahead)
    back_high, back_low = halves(back)
    return (
        np.concatenate([first_high, first_low], 1),
        turn,
        np.concatenate([ahead_high, ahead_high, ahead_low], 0),
        np.concatenate([back_high, back_high, back_low], 0),
        np.concatenate([last_high, last_high, last_low], 1),
    )


def dot(left, right):
    return jnp.dot(left, right, preferred_element_type=jnp.float32)


def split(value):
    high = value.astype(jnp.bfloat16)
    return high, (value - high.astype(jnp.float32)).astype(jnp.bfloat16)


def params():
    return pltpu.CompilerParams(vmem_limit_bytes=VMEM)


def whole():
    return pl.BlockSpec(memory_space=pltpu.VMEM)


def prepare_kernel(far, key_ref, value_ref, filter_ref, out_ref):
    core = lax.axis_index("core")
    half = 1 - core if far else core
    columns = pl.ds(pl.multiple_of(half * HALF, HALF), HALF)
    source = key_ref[:, columns].astype(jnp.float32) * value_ref[:, columns].astype(jnp.float32)
    source = source.T.reshape(BLOCKS, SLICE, BLOCK)
    taps = filter_ref[:, columns].T.reshape(BLOCKS, SLICE, BLOCK)
    out_ref[...] = jnp.concatenate([source, taps], 1).astype(jnp.bfloat16)


def prepare(far, key, value, taps):
    return pl.pallas_call(
        functools.partial(prepare_kernel, far),
        out_shape=jax.ShapeDtypeStruct((BLOCKS, 2 * SLICE, BLOCK), jnp.bfloat16),
        in_specs=[whole()] * 3,
        out_specs=whole(),
        compiler_params=params(),
        name="prepare_far" if far else "prepare_near",
    )(key, value, taps)


def turn_kernel(query_ref, near_ref, far_ref):
    core = lax.axis_index("core")
    for half, ref in ((core, near_ref), (1 - core, far_ref)):
        columns = pl.ds(pl.multiple_of(half * HALF, HALF), HALF)
        ref[...] = query_ref[:, columns].astype(jnp.float32).T.astype(jnp.bfloat16)


def turn_query(query):
    return pl.pallas_call(
        turn_kernel,
        out_shape=[jax.ShapeDtypeStruct((HALF, BLOCK), jnp.bfloat16)] * 2,
        in_specs=[whole()],
        out_specs=[whole()] * 2,
        compiler_params=params(),
        name="turn_query",
    )(query)


def convolve_kernel(got_ref, own_ref, other_ref, first_ref, turn_ref, ahead_ref, back_ref, last_ref, out_ref):
    core, near = lax.axis_index("core"), lax.axis_index("zl")
    place = lax.axis_index("x") * 8 + lax.axis_index("zh") * 2 + near
    cos_t = turn_ref[0][:, None, :]
    sin_t = turn_ref[1][:, None, :]
    rows = STEPS * SLICE

    def turned(real, imag, sign):
        real = real.reshape(STEPS, SLICE, INNER)
        imag = imag.reshape(STEPS, SLICE, INNER)
        one = real * cos_t - (sign * imag) * sin_t
        two = imag * cos_t + (sign * real) * sin_t
        return one.reshape(rows, INNER), two.reshape(rows, INNER)

    outs = []
    for s in range(2):
        got = got_ref[:, s].astype(jnp.float32).reshape(16, 2, 2, SLICE, BLOCK)
        source = got[:, :, 0].reshape(BLOCKS * SLICE, BLOCK)
        taps = got[:, :, 1].reshape(BLOCKS * SLICE, BLOCK)
        both = jnp.concatenate(
            [
                jnp.concatenate([source[:, :INNER], taps[:, :INNER]], 1),
                jnp.concatenate([source[:, INNER:], taps[:, INNER:]], 1),
            ],
            0,
        ).astype(jnp.bfloat16)
        first = dot(first_ref[...], jnp.concatenate([both, both], 0))
        spectra = []
        for part in range(2):
            columns = slice(part * INNER, (part + 1) * INNER)
            real, imag = turned(first[:rows, columns], first[rows:, columns], -1.0)
            high, low = split(jnp.concatenate([real, imag], 1))
            spectra.append(dot(jnp.concatenate([high, low, high], 1), ahead_ref[...]))
        (ar, ai), (br, bi) = [(z[:, :INNER], z[:, INNER:]) for z in spectra]
        product = jnp.concatenate([ar * br - ai * bi, ar * bi + ai * br], 1)
        high, low = split(product)
        inner = dot(jnp.concatenate([high, low, high], 1), back_ref[...])
        real, imag = turned(inner[:, :INNER], inner[:, INNER:], 1.0)
        high, low = split(jnp.concatenate([real, imag], 0))
        conv = dot(last_ref[...], jnp.concatenate([high, low, high], 0))
        conv = jnp.concatenate([conv[: BLOCKS * SLICE], conv[BLOCKS * SLICE :]], 1)
        channel = core * HALF + place * SLICE + lax.broadcasted_iota(jnp.int32, (SLICE, BLOCK), 0)
        picked = channel == lax.broadcasted_iota(jnp.int32, (SLICE, BLOCK), 1)
        gains = jnp.where(near == s, own_ref[...], other_ref[...])
        gain = jnp.sum(jnp.where(picked, gains, 0.0), 1, keepdims=True)
        total = conv.reshape(BLOCKS, SLICE, BLOCK) + gain[None] * source.reshape(BLOCKS, SLICE, BLOCK)
        outs.append(total)
    out_ref[...] = jnp.concatenate(outs, 1).astype(jnp.bfloat16)


def convolve(got, own_gain, other_gain):
    return pl.pallas_call(
        convolve_kernel,
        out_shape=jax.ShapeDtypeStruct((BLOCKS, 2 * SLICE, BLOCK), jnp.bfloat16),
        in_specs=[whole()] * 8,
        out_specs=whole(),
        compiler_params=params(),
        name="convolve",
    )(got, own_gain, other_gain, *tables())


def gate_kernel(conv_ref, near_ref, sibling_ref, crossed_ref, out_ref):
    core, line = lax.axis_index("core"), lax.axis_index("zl")
    kept = jnp.where(core == line, near_ref[...].astype(jnp.float32), sibling_ref[...].astype(jnp.float32))
    crossed = crossed_ref[...].astype(jnp.float32)
    conv = conv_ref[...].astype(jnp.float32).reshape(BLOCKS, 2, SLICE, BLOCK)
    for s in range(2):
        query = jnp.where(line == s, kept, crossed)
        gated = query * conv[:, s].reshape(HALF, BLOCK)
        out_ref[:, s * HALF : (s + 1) * HALF] = gated.T.astype(jnp.bfloat16)


def gate(conv, near, sibling, crossed):
    return pl.pallas_call(
        gate_kernel,
        out_shape=jax.ShapeDtypeStruct((BLOCK, BLOCK), jnp.bfloat16),
        in_specs=[whole()] * 4,
        out_specs=whole(),
        compiler_params=params(),
        name="gate",
    )(conv, near, sibling, crossed)


def project_kernel(*refs):
    pieces, weight_ref, out_ref = refs[:8], refs[8], refs[9]
    core, y = lax.axis_index("core"), lax.axis_index("y")
    total = None
    for index, piece in enumerate(pieces):
        back, sibling = index // 2, index % 2
        owner = lax.rem(y + 4 - back, 4)
        side = 1 - core if sibling else core
        for s in range(2):
            start = pl.multiple_of(owner * 1024 + s * 512 + side * HALF, HALF)
            term = dot(piece[:, s * HALF : (s + 1) * HALF], weight_ref[pl.ds(start, HALF), :])
            total = term if total is None else total + term
    out_ref[...] = total.astype(jnp.bfloat16)


def project(pieces, weight):
    return pl.pallas_call(
        project_kernel,
        out_shape=jax.ShapeDtypeStruct((BLOCK, BLOCK), jnp.bfloat16),
        in_specs=[whole()] * 9,
        out_specs=whole(),
        compiler_params=params(),
        name="project",
    )(*pieces, weight)


def on_device(query, key, value, taps, gain, weight):
    core, line = lax.axis_index("core"), lax.axis_index("zl")
    weight = lax.ppermute(weight, ("core", "zl"), SWAP)
    weight = lax.all_gather(weight, LINE, axis=0, tiled=True)
    far = prepare(True, key, value, taps)
    arrived = lax.ppermute(far, "core", PAIR)
    near = prepare(False, key, value, taps)
    blocks = jnp.where(core == 0, jnp.stack([near, arrived], 1), jnp.stack([arrived, near], 1))
    got = lax.all_to_all(blocks, LINE, 0, 0, tiled=True)
    got = got.reshape(16, 2, 2, 2 * SLICE, BLOCK)
    gain = gain.reshape(1, BLOCK)
    other_gain = lax.ppermute(gain, "zl", PAIR)
    query_near, query_far = turn_query(query)
    sibling = lax.ppermute(query_far, "core", PAIR)
    crossing = jnp.where(core == line, sibling, query_near)
    crossed = lax.ppermute(crossing, "zl", PAIR)
    conv = convolve(got, gain, other_gain)
    conv = lax.all_to_all(conv, LINE, 0, 0, tiled=True)
    gated = gate(conv, query_near, sibling, crossed)
    pieces = [gated] + [lax.ppermute(gated, "y", [(i, (i + k) % 4) for i in range(4)]) for k in (1, 2, 3)]
    both = []
    for piece in pieces:
        both += [piece, lax.ppermute(piece, "core", PAIR)]
    mixed = project(both, weight)
    return lax.ppermute(mixed, ("core", "zl"), SWAP)


def solution(mesh):
    fine = Mesh(mesh.devices.reshape(4, 4, 2, 4, 2), AXES)
    rows, columns = ("x", "zh", "core"), ("y", "zl")
    placed = P(rows, columns)
    return jax.shard_map(
        on_device,
        mesh=fine,
        in_specs=(placed, placed, placed, placed, P(columns), placed),
        out_specs=placed,
        check_vma=False,
    )
```

```python
import functools
import math

import jax
import jax.numpy as jnp
import numpy as np
from jax import lax
from jax.experimental import pallas as pl
from jax.experimental.pallas import tpu as pltpu
from jax.sharding import Mesh
from jax.sharding import PartitionSpec as P

AXES = ("x", "zh", "core", "y", "zl")
LINE = ("x", "zh", "zl")
BLOCKS = 32
BLOCK = 512
SLICE = 8
HALF = 256
STEPS = 64
INNER = 256
PERIOD = 32768
SWAP = [(0, 0), (1, 2), (2, 1), (3, 3)]
PAIR = [(0, 1), (1, 0)]
ROWS = [(4 * h + 2 * a + b, 4 * h + 2 * b + a) for h in range(2) for a in range(2) for b in range(2)]


def halves(table):
    high = table.astype(np.float32).astype(jnp.bfloat16)
    low = (table - high.astype(np.float64)).astype(np.float32).astype(jnp.bfloat16)
    return high, low


def tables():
    odd = np.arange(STEPS) + 0.5
    steps = np.arange(STEPS)
    inner = np.arange(INNER)
    outer = 2 * math.pi * np.outer(odd, steps) / (2 * STEPS)
    same = np.eye(SLICE)
    order = steps.reshape(BLOCKS, 2).T.reshape(-1)
    cos_o, sin_o = np.cos(outer)[:, order], np.sin(outer)[:, order]
    first = np.concatenate([np.kron(cos_o, same), np.kron(-sin_o, same)], 0)
    last = np.concatenate([np.kron(cos_o.T, same), np.kron(-sin_o.T, same)], 1) / (PERIOD // 2)
    turn = 2 * math.pi * np.outer(odd, inner) / PERIOD
    turn = np.stack([np.cos(turn), np.sin(turn)]).astype(np.float32)
    angle = 2 * math.pi * (np.outer(inner, inner) % INNER) / INNER
    cos_i, sin_i = np.cos(angle), np.sin(angle)
    ahead = np.block([[cos_i, -sin_i], [sin_i, cos_i]])
    back = np.block([[cos_i, sin_i], [-sin_i, cos_i]])
    first_high, first_low = halves(first)
    last_high, last_low = halves(last)
    ahead_high, ahead_low = halves(ahead)
    back_high, back_low = halves(back)
    return (
        np.concatenate([first_high, first_low], 1),
        turn,
        np.concatenate([ahead_high, ahead_high, ahead_low], 0),
        np.concatenate([back_high, back_high, back_low], 0),
        np.concatenate([last_high, last_high, last_low], 1),
    )


def dot(left, right):
    return jnp.dot(left, right, preferred_element_type=jnp.float32)


def split(value):
    high = value.astype(jnp.bfloat16)
    return high, (value - high.astype(jnp.float32)).astype(jnp.bfloat16)


def params(mebibytes):
    return pltpu.CompilerParams(vmem_limit_bytes=mebibytes * 1024 * 1024)


def whole():
    return pl.BlockSpec(memory_space=pltpu.VMEM)


def anywhere():
    return pl.BlockSpec(memory_space=pl.ANY)


def prepare_kernel(key_hbm, value_hbm, filter_hbm, out_hbm, key_ref, value_ref, filter_ref, out_ref, sems, out_sems):
    moves = []
    for i in range(4):
        columns = pl.ds(i * 128, 128)
        for j, (far, near) in enumerate(((key_hbm, key_ref), (value_hbm, value_ref), (filter_hbm, filter_ref))):
            moves.append(pltpu.make_async_copy(far.at[:, columns], near.at[i], sems.at[i, j]))
            moves[-1].start()
    outs = []
    for i in range(4):
        for move in moves[3 * i : 3 * i + 3]:
            move.wait()
        source = key_ref[i].astype(jnp.float32) * value_ref[i].astype(jnp.float32)
        source = source.T.reshape(8, 2, SLICE, BLOCK)
        taps = filter_ref[i].T.reshape(8, 2, SLICE, BLOCK)
        out_ref[i] = jnp.concatenate([source, taps], 2).astype(jnp.bfloat16)
        place = out_hbm.at[pl.ds((i % 2) * 8, 8), i // 2]
        outs.append(pltpu.make_async_copy(out_ref.at[i], place, out_sems.at[i]))
        outs[-1].start()
    for out in outs:
        out.wait()


def prepare(key, value, taps):
    return pl.pallas_call(
        prepare_kernel,
        out_shape=jax.ShapeDtypeStruct((16, 2, 2, 2 * SLICE, BLOCK), jnp.bfloat16),
        in_specs=[anywhere()] * 3,
        out_specs=anywhere(),
        scratch_shapes=[
            pltpu.VMEM((4, BLOCK, 128), jnp.bfloat16),
            pltpu.VMEM((4, BLOCK, 128), jnp.bfloat16),
            pltpu.VMEM((4, BLOCK, 128), jnp.float32),
            pltpu.VMEM((4, 8, 2, 2 * SLICE, BLOCK), jnp.bfloat16),
            pltpu.SemaphoreType.DMA((4, 3)),
            pltpu.SemaphoreType.DMA((4,)),
        ],
        compiler_params=params(56),
        name="prepare",
    )(key, value, taps)


def turn_kernel(query_ref, near_ref, far_ref):
    core = lax.axis_index("core")
    for half, ref in ((core, near_ref), (1 - core, far_ref)):
        columns = pl.ds(pl.multiple_of(half * HALF, HALF), HALF)
        ref[...] = query_ref[:, columns].astype(jnp.float32).T.astype(jnp.bfloat16)


def turn_query(query):
    return pl.pallas_call(
        turn_kernel,
        out_shape=[jax.ShapeDtypeStruct((HALF, BLOCK), jnp.bfloat16)] * 2,
        in_specs=[whole()],
        out_specs=[whole()] * 2,
        compiler_params=params(16),
        name="turn_query",
    )(query)


def convolve_kernel(got_ref, own_ref, other_ref, turn_ref, *refs):
    out_ref, tables_here, sems = refs[4], refs[5:9], refs[9]
    copies = [pltpu.make_async_copy(refs[i], tables_here[i], sems.at[i]) for i in range(4)]
    for copy in copies:
        copy.start()
    first_ref, ahead_ref, back_ref, last_ref = tables_here
    core, near = lax.axis_index("core"), lax.axis_index("zl")
    place = lax.axis_index("x") * 8 + lax.axis_index("zh") * 2 + near
    cos_t = turn_ref[0][:, None, :]
    sin_t = turn_ref[1][:, None, :]
    rows = STEPS * SLICE

    def turned(real, imag, sign):
        real = real.reshape(STEPS, SLICE, INNER)
        imag = imag.reshape(STEPS, SLICE, INNER)
        one = real * cos_t - (sign * imag) * sin_t
        two = imag * cos_t + (sign * real) * sin_t
        return one.reshape(rows, INNER), two.reshape(rows, INNER)

    outs = []
    for s in range(2):
        got = got_ref[:, :, s].astype(jnp.float32).reshape(16, 2, 2, SLICE, BLOCK)
        source = got[:, :, 0].reshape(BLOCKS * SLICE, BLOCK)
        taps = got[:, :, 1].reshape(BLOCKS * SLICE, BLOCK)
        both = jnp.concatenate(
            [
                jnp.concatenate([source[:, :INNER], taps[:, :INNER]], 1),
                jnp.concatenate([source[:, INNER:], taps[:, INNER:]], 1),
            ],
            0,
        ).astype(jnp.bfloat16)
        if s == 0:
            copies[0].wait()
        first = dot(first_ref[...], jnp.concatenate([both, both], 0))
        if s == 0:
            copies[1].wait()
        spectra = []
        for part in range(2):
            columns = slice(part * INNER, (part + 1) * INNER)
            real, imag = turned(first[:rows, columns], first[rows:, columns], -1.0)
            high, low = split(jnp.concatenate([real, imag], 1))
            spectra.append(dot(jnp.concatenate([high, low, high], 1), ahead_ref[...]))
        (ar, ai), (br, bi) = [(z[:, :INNER], z[:, INNER:]) for z in spectra]
        product = jnp.concatenate([ar * br - ai * bi, ar * bi + ai * br], 1)
        high, low = split(product)
        if s == 0:
            copies[2].wait()
        inner = dot(jnp.concatenate([high, low, high], 1), back_ref[...])
        real, imag = turned(inner[:, :INNER], inner[:, INNER:], 1.0)
        high, low = split(jnp.concatenate([real, imag], 0))
        if s == 0:
            copies[3].wait()
        conv = dot(last_ref[...], jnp.concatenate([high, low, high], 0))
        conv = jnp.concatenate([conv[: BLOCKS * SLICE], conv[BLOCKS * SLICE :]], 1)
        channel = core * HALF + place * SLICE + lax.broadcasted_iota(jnp.int32, (SLICE, BLOCK), 0)
        picked = channel == lax.broadcasted_iota(jnp.int32, (SLICE, BLOCK), 1)
        gains = jnp.where(near == s, own_ref[...], other_ref[...])
        gain = jnp.sum(jnp.where(picked, gains, 0.0), 1, keepdims=True)
        total = conv.reshape(BLOCKS, SLICE, BLOCK) + gain[None] * source.reshape(BLOCKS, SLICE, BLOCK)
        outs.append(total)
    out_ref[...] = jnp.concatenate(outs, 1).astype(jnp.bfloat16)


def convolve(got, own_gain, other_gain):
    first, turn, ahead, back, last = tables()
    return pl.pallas_call(
        convolve_kernel,
        out_shape=jax.ShapeDtypeStruct((BLOCKS, 2 * SLICE, BLOCK), jnp.bfloat16),
        in_specs=[whole()] * 4 + [pl.BlockSpec(memory_space=pl.ANY)] * 4,
        out_specs=whole(),
        scratch_shapes=[pltpu.VMEM(table.shape, jnp.bfloat16) for table in (first, ahead, back, last)]
        + [pltpu.SemaphoreType.DMA((4,))],
        compiler_params=params(56),
        name="convolve",
    )(got, own_gain, other_gain, turn, first, ahead, back, last)


def gate_kernel(conv_ref, near_ref, sibling_ref, crossed_ref, out_ref):
    core, line = lax.axis_index("core"), lax.axis_index("zl")
    kept = jnp.where(core == line, near_ref[...].astype(jnp.float32), sibling_ref[...].astype(jnp.float32))
    crossed = crossed_ref[...].astype(jnp.float32)
    conv = conv_ref[...].astype(jnp.float32).reshape(BLOCKS, 2, SLICE, BLOCK)
    for s in range(2):
        query = jnp.where(line == s, kept, crossed)
        gated = query * conv[:, s].reshape(HALF, BLOCK)
        out_ref[:, s * HALF : (s + 1) * HALF] = gated.T.astype(jnp.bfloat16)


def gate(conv, near, sibling, crossed):
    return pl.pallas_call(
        gate_kernel,
        out_shape=jax.ShapeDtypeStruct((BLOCK, BLOCK), jnp.bfloat16),
        in_specs=[whole()] * 4,
        out_specs=whole(),
        compiler_params=params(16),
        name="gate",
    )(conv, near, sibling, crossed)


def project_kernel(own_ref, after_ref, ahead_ref, *refs):
    weights, (top_ref, low_ref, last_ref, held, sems) = refs[:5], refs[5:]
    x, y = lax.axis_index("x"), lax.axis_index("y")
    first, second = pl.ds(0, 2), pl.ds(2, 2)
    parts = [(weights[0].at[first], weights[0].at[second]), (weights[1].at[first], weights[1].at[second])]
    parts += [(weights[2], weights[3]), (weights[4].at[first], weights[4].at[second])]
    steps = (0, 1, 3, 2)
    for index, back in enumerate(steps):
        away = lax.rem(x - y + back + 4, 4)
        for number, pair in enumerate(parts):

            @pl.when(away == number)
            def _():
                for half in range(2):
                    pltpu.make_async_copy(pair[half], held.at[index, half], sems.at[index, half]).start()

    pieces = (own_ref, after_ref, ahead_ref)
    totals = [None, None]
    for index in range(4):
        for half in range(2):
            pltpu.make_async_copy(weights[2], held.at[index, half], sems.at[index, half]).wait()
        for side in range(2):
            block = held[index, :, :, side].reshape(BLOCK, BLOCK)
            if index < 3:
                term = dot(pieces[index][...], block)
                totals[side] = term if totals[side] is None else totals[side] + term
            else:
                last_ref[side] = block
    for side in range(2):
        top_ref[side] = totals[side][:HALF]
        low_ref[side] = totals[side][HALF:]


def project(pieces, weights):
    part = jax.ShapeDtypeStruct((2, HALF, BLOCK), jnp.float32)
    return pl.pallas_call(
        project_kernel,
        out_shape=[part, part, jax.ShapeDtypeStruct((2, BLOCK, BLOCK), jnp.bfloat16)],
        in_specs=[whole()] * 3 + [anywhere()] * 5,
        out_specs=[whole()] * 3,
        scratch_shapes=[
            pltpu.VMEM((4, 2, 2, 2, 128, BLOCK), jnp.bfloat16),
            pltpu.SemaphoreType.DMA((4, 2)),
        ],
        compiler_params=params(24),
        cost_estimate=pl.CostEstimate(flops=6 * BLOCK * BLOCK * 1024, bytes_accessed=8 * 2**20, transcendentals=0),
        name="project",
    )(*pieces, *weights)


def finish_kernel(piece_ref, before_ref, weight_ref, keep_ref, send_ref):
    core = lax.axis_index("core")
    for side, ref in ((core, keep_ref), (1 - core, send_ref)):
        ref[...] = before_ref[side] + dot(piece_ref[...], weight_ref[side])


def finish(piece, before, weight):
    return pl.pallas_call(
        finish_kernel,
        out_shape=[jax.ShapeDtypeStruct((HALF, BLOCK), jnp.float32)] * 2,
        in_specs=[whole()] * 3,
        out_specs=[whole()] * 2,
        compiler_params=params(16),
        name="finish",
    )(piece, before, weight)


def along(steps):
    return [(i, (i + steps) % 4) for i in range(4)]


def cross(value):
    return lax.ppermute(value, "core", PAIR)


def on_device(query, key, value, taps, gain, weight):
    core, line = lax.axis_index("core"), lax.axis_index("zl")
    weight = lax.ppermute(weight, ("zh", "core"), ROWS)
    blocks = prepare(key, value, taps)
    blocks, weight = lax.optimization_barrier((blocks, weight))
    weight = lax.all_gather(weight, ("zh", "zl"), axis=0, tiled=True)
    got = lax.all_to_all(blocks.reshape(64, 2 * SLICE, BLOCK), ("x", "zh", "core", "zl"), 0, 0, tiled=True)
    got = got.reshape(16, 2, 2, 2 * SLICE, BLOCK)
    gain, query, _ = lax.optimization_barrier((gain, query, blocks))
    gain = gain.reshape(1, BLOCK)
    other_gain = lax.ppermute(gain, "zl", PAIR)
    query_near, query_far = turn_query(query)
    sibling = cross(query_far)
    crossing = jnp.where(core == line, sibling, query_near)
    crossed = lax.ppermute(crossing, "zl", PAIR)
    conv = convolve(got, gain, other_gain)
    weight, _ = lax.optimization_barrier((weight, conv))
    weight = weight.reshape(4, 2, 128, BLOCK)
    weight_1 = lax.ppermute(weight, "x", along(1))
    weight_3 = lax.ppermute(weight, "x", along(3))
    weight_top = lax.ppermute(weight_1[:2], "x", along(1))
    weight_low = lax.ppermute(weight_3[2:], "x", along(3))
    weights = (weight, weight_1, weight_top, weight_low, weight_3)
    conv = lax.all_to_all(conv, LINE, 0, 0, tiled=True)
    gated = gate(conv, query_near, sibling, crossed)
    after = lax.ppermute(gated, "y", along(1))
    ahead = lax.ppermute(gated, "y", along(3))
    upper = lax.ppermute(after[:HALF], "y", along(1))
    lower = lax.ppermute(ahead[HALF:], "y", along(3))
    top, low, last = project([gated, after, ahead], weights)
    mixed = []
    for part, piece in ((top, upper), (low, lower)):
        keep, send = finish(piece, part, last)
        done = (keep + cross(send)).astype(jnp.bfloat16)
        mixed.append(lax.ppermute(done, ("core", "zl"), SWAP))
    return jnp.concatenate(mixed, 0)


def solution(mesh):
    fine = Mesh(mesh.devices.reshape(4, 4, 2, 4, 2), AXES)
    rows, columns = ("x", "zh", "core"), ("y", "zl")
    placed = P(rows, columns)
    return jax.shard_map(
        on_device,
        mesh=fine,
        in_specs=(placed, placed, placed, placed, P(columns), placed),
        out_specs=placed,
        check_vma=False,
    )
```

```python
import functools
import math

import jax
import jax.numpy as jnp
import numpy as np
from jax import lax
from jax.experimental import pallas as pl
from jax.experimental.pallas import tpu as pltpu
from jax.sharding import Mesh
from jax.sharding import PartitionSpec as P

AXES = ("x", "zh", "core", "y", "zl")
TOKENS = ("x", "zh", "core")
BLOCKS = 32
BLOCK = 512
CHANNELS = 16
SLICE = 8
HALF = 256
STEPS = 64
INNER = 256
PERIOD = 32768
PAIR = [(0, 1), (1, 0)]


def halves(table):
    high = table.astype(np.float32).astype(jnp.bfloat16)
    low = (table - high.astype(np.float64)).astype(np.float32).astype(jnp.bfloat16)
    return high, low


def tables():
    odd = np.arange(STEPS) + 0.5
    steps = np.arange(STEPS)
    inner = np.arange(INNER)
    outer = 2 * math.pi * np.outer(odd, steps) / (2 * STEPS)
    same = np.eye(SLICE)
    order = steps.reshape(BLOCKS, 2).T.reshape(-1)
    cos_o, sin_o = np.cos(outer)[:, order], np.sin(outer)[:, order]
    first = np.concatenate([np.kron(cos_o, same), np.kron(-sin_o, same)], 0)
    last = np.concatenate([np.kron(cos_o.T, same), np.kron(-sin_o.T, same)], 1) / (PERIOD // 2)
    turn = 2 * math.pi * np.outer(odd, inner) / PERIOD
    turn = np.stack([np.cos(turn), np.sin(turn)]).astype(np.float32)
    angle = 2 * math.pi * (np.outer(inner, inner) % INNER) / INNER
    cos_i, sin_i = np.cos(angle), np.sin(angle)
    ahead = np.block([[cos_i, -sin_i], [sin_i, cos_i]])
    back = np.block([[cos_i, sin_i], [-sin_i, cos_i]])
    first_high, first_low = halves(first)
    last_high, last_low = halves(last)
    ahead_high, ahead_low = halves(ahead)
    back_high, back_low = halves(back)
    return (
        np.concatenate([first_high, first_low], 1),
        turn,
        np.concatenate([ahead_high, ahead_low], 0),
        np.concatenate([back_high, back_low], 0),
        np.concatenate([last_high, last_low], 1),
    )


def dot(left, right):
    return jnp.dot(left, right, preferred_element_type=jnp.float32)


def split(value):
    high = value.astype(jnp.bfloat16)
    return high, (value - high.astype(jnp.float32)).astype(jnp.bfloat16)


def params(mebibytes):
    return pltpu.CompilerParams(vmem_limit_bytes=mebibytes * 1024 * 1024)


def whole():
    return pl.BlockSpec(memory_space=pltpu.VMEM)


def anywhere():
    return pl.BlockSpec(memory_space=pl.ANY)


def prepare_kernel(key_hbm, value_hbm, filter_hbm, out_hbm, key_ref, value_ref, filter_ref, out_ref, sems, out_sems):
    moves = []
    for i in range(4):
        columns = pl.ds(i * 128, 128)
        for j, (far, near) in enumerate(((key_hbm, key_ref), (value_hbm, value_ref), (filter_hbm, filter_ref))):
            moves.append(pltpu.make_async_copy(far.at[:, columns], near.at[i], sems.at[i, j]))
            moves[-1].start()
    outs = []
    for i in range(4):
        for move in moves[3 * i : 3 * i + 3]:
            move.wait()
        source = key_ref[i].astype(jnp.float32) * value_ref[i].astype(jnp.float32)
        source = source.T.reshape(8, CHANNELS, BLOCK)
        taps = filter_ref[i].T.reshape(8, CHANNELS, BLOCK)
        out_ref[i] = jnp.concatenate([source, taps], 1).astype(jnp.bfloat16)
        outs.append(pltpu.make_async_copy(out_ref.at[i], out_hbm.at[pl.ds(i * 8, 8)], out_sems.at[i]))
        outs[-1].start()
    for out in outs:
        out.wait()


def prepare(key, value, taps):
    return pl.pallas_call(
        prepare_kernel,
        out_shape=jax.ShapeDtypeStruct((BLOCKS, 2 * CHANNELS, BLOCK), jnp.bfloat16),
        in_specs=[anywhere()] * 3,
        out_specs=anywhere(),
        scratch_shapes=[
            pltpu.VMEM((4, BLOCK, 128), jnp.bfloat16),
            pltpu.VMEM((4, BLOCK, 128), jnp.bfloat16),
            pltpu.VMEM((4, BLOCK, 128), jnp.float32),
            pltpu.VMEM((4, 8, 2 * CHANNELS, BLOCK), jnp.bfloat16),
            pltpu.SemaphoreType.DMA((4, 3)),
            pltpu.SemaphoreType.DMA((4,)),
        ],
        compiler_params=params(56),
        name="prepare",
    )(key, value, taps)


def thrice(table_ref):
    return jnp.concatenate([table_ref[:BLOCK], table_ref[...]], 0)


def convolve_kernel(got_ref, gain_ref, turn_ref, *refs):
    out_ref, tables_here, sems = refs[4], refs[5:9], refs[9]
    copies = []
    for i in range(4):
        part = refs[i].shape[0] // 4
        for j in range(4):
            rows = pl.ds(j * part, part)
            copies.append(pltpu.make_async_copy(refs[i].at[rows], tables_here[i].at[rows], sems.at[i, j]))
            copies[-1].start()

    def arrived(i):
        for copy in copies[4 * i : 4 * i + 4]:
            copy.wait()

    first_ref, ahead_ref, back_ref, last_ref = tables_here
    place = lax.axis_index("x") * 8 + lax.axis_index("zh") * 2 + lax.axis_index("core")
    cos_t = turn_ref[0][:, None, :]
    sin_t = turn_ref[1][:, None, :]
    rows = STEPS * SLICE

    def turned(real, imag, sign):
        real = real.reshape(STEPS, SLICE, INNER)
        imag = imag.reshape(STEPS, SLICE, INNER)
        one = real * cos_t - (sign * imag) * sin_t
        two = imag * cos_t + (sign * real) * sin_t
        return one.reshape(rows, INNER), two.reshape(rows, INNER)

    outs = []
    for s in range(2):
        got = got_ref[...].astype(jnp.float32).reshape(BLOCKS, 2, 2, SLICE, BLOCK)
        source = got[:, 0, s].reshape(BLOCKS * SLICE, BLOCK)
        taps = got[:, 1, s].reshape(BLOCKS * SLICE, BLOCK)
        both = jnp.concatenate(
            [
                jnp.concatenate([source[:, :INNER], taps[:, :INNER]], 1),
                jnp.concatenate([source[:, INNER:], taps[:, INNER:]], 1),
            ],
            0,
        ).astype(jnp.bfloat16)
        if s == 0:
            arrived(0)
        first = dot(first_ref[...], jnp.concatenate([both, both], 0))
        if s == 0:
            arrived(1)
        spectra = []
        for part in range(2):
            columns = slice(part * INNER, (part + 1) * INNER)
            real, imag = turned(first[:rows, columns], first[rows:, columns], -1.0)
            high, low = split(jnp.concatenate([real, imag], 1))
            spectra.append(dot(jnp.concatenate([high, low, high], 1), thrice(ahead_ref)))
        (ar, ai), (br, bi) = [(z[:, :INNER], z[:, INNER:]) for z in spectra]
        product = jnp.concatenate([ar * br - ai * bi, ar * bi + ai * br], 1)
        high, low = split(product)
        if s == 0:
            arrived(2)
        inner = dot(jnp.concatenate([high, low, high], 1), thrice(back_ref))
        real, imag = turned(inner[:, :INNER], inner[:, INNER:], 1.0)
        high, low = split(jnp.concatenate([real, imag], 0))
        if s == 0:
            arrived(3)
        conv = dot(jnp.concatenate([last_ref[:, :1024], last_ref[...]], 1), jnp.concatenate([high, low, high], 0))
        conv = jnp.concatenate([conv[: BLOCKS * SLICE], conv[BLOCKS * SLICE :]], 1)
        channel = place * CHANNELS + s * SLICE + lax.broadcasted_iota(jnp.int32, (SLICE, BLOCK), 0)
        picked = channel == lax.broadcasted_iota(jnp.int32, (SLICE, BLOCK), 1)
        gain = jnp.sum(jnp.where(picked, gain_ref[...], 0.0), 1, keepdims=True)
        total = conv.reshape(BLOCKS, SLICE, BLOCK) + gain[None] * source.reshape(BLOCKS, SLICE, BLOCK)
        outs.append(total)
    out_ref[...] = jnp.concatenate(outs, 1).astype(jnp.bfloat16)


def convolve(got, gain):
    first, turn, ahead, back, last = tables()
    return pl.pallas_call(
        convolve_kernel,
        out_shape=jax.ShapeDtypeStruct((BLOCKS, CHANNELS, BLOCK), jnp.bfloat16),
        in_specs=[whole()] * 3 + [anywhere()] * 4,
        out_specs=whole(),
        scratch_shapes=[pltpu.VMEM(table.shape, jnp.bfloat16) for table in (first, ahead, back, last)]
        + [pltpu.SemaphoreType.DMA((4, 4))],
        compiler_params=params(56),
        name="convolve",
    )(got, gain, turn, first, ahead, back, last)


def gate_kernel(conv_ref, query_ref, out_ref, top_ref, low_ref):
    conv = conv_ref[...].astype(jnp.float32).reshape(BLOCK, BLOCK).T
    gated = (query_ref[...].astype(jnp.float32) * conv).astype(jnp.bfloat16)
    out_ref[...] = gated
    top_ref[...] = gated[:HALF]
    low_ref[...] = gated[HALF:]


def gate(conv, query):
    half = jax.ShapeDtypeStruct((HALF, BLOCK), jnp.bfloat16)
    return pl.pallas_call(
        gate_kernel,
        out_shape=[jax.ShapeDtypeStruct((BLOCK, BLOCK), jnp.bfloat16), half, half],
        in_specs=[whole()] * 2,
        out_specs=[whole()] * 3,
        compiler_params=params(16),
        name="gate",
    )(conv, query)


def order_kernel(own_ref, sibling_ref, *refs):
    outs, sems = refs[:4], refs[4]
    core, x, y, zh = (lax.axis_index(axis) for axis in ("core", "x", "y", "zh"))
    moves = []
    for back, out in enumerate(outs):
        away = lax.rem(x - y + back + 4, 4)
        for k in range(4):
            place = 2 * lax.rem(zh + 4 - k, 4)
            moves.append(pltpu.make_async_copy(own_ref.at[away, k], out.at[place + core], sems.at[back, k, 0]))
            moves.append(pltpu.make_async_copy(sibling_ref.at[away, k], out.at[place + 1 - core], sems.at[back, k, 1]))
    for move in moves:
        move.start()
    for move in moves:
        move.wait()


def order(own, sibling):
    return pl.pallas_call(
        order_kernel,
        out_shape=[jax.ShapeDtypeStruct((8, 128, BLOCK), jnp.bfloat16)] * 4,
        in_specs=[anywhere()] * 2,
        out_specs=[anywhere()] * 4,
        scratch_shapes=[pltpu.SemaphoreType.DMA((4, 4, 2))],
        compiler_params=params(16),
        name="order",
    )(own, sibling)


def rows_of(weight_ref, column):
    start = pl.multiple_of(column * 4, 4)
    return weight_ref[pl.ds(start, 4)].reshape(BLOCK, BLOCK)


def project_kernel(sides, begins, *refs):
    count = len(sides)
    weights, pieces = refs[:count], refs[count:-1]
    line = lax.axis_index("zl")
    totals = [None, None] if begins else [refs[-2][:HALF], refs[-2][HALF:]]
    for side, weight in zip(sides, weights):
        if pieces[0].shape[0] == BLOCK:
            parts, pieces = [pieces[0][:HALF], pieces[0][HALF:]], pieces[1:]
        else:
            parts, pieces = [pieces[0][...], pieces[1][...]], pieces[2:]
        rows = rows_of(weight, 1 - line if side else line)
        for half in range(2):
            term = dot(parts[half], rows)
            totals[half] = term if totals[half] is None else totals[half] + term
    refs[-1][:HALF] = totals[0]
    refs[-1][HALF:] = totals[1]


def project(sides, pieces, weights, before=None):
    count = len(weights)
    operands = list(weights) + list(pieces) + ([] if before is None else [before])
    return pl.pallas_call(
        functools.partial(project_kernel, sides, before is None),
        out_shape=jax.ShapeDtypeStruct((BLOCK, BLOCK), jnp.float32),
        in_specs=[whole()] * len(operands),
        out_specs=whole(),
        compiler_params=params(16),
        cost_estimate=pl.CostEstimate(
            flops=2 * count * BLOCK**3, bytes_accessed=(count + 2) * 2**20, transcendentals=0
        ),
        name="project",
    )(*operands)


def finish_kernel(upper_ref, lower_ref, upper_far_ref, lower_far_ref, weight_ref, before_ref, out_ref):
    line = lax.axis_index("zl")
    near, far = rows_of(weight_ref, line), rows_of(weight_ref, 1 - line)
    for start, piece, piece_far in ((0, upper_ref, upper_far_ref), (HALF, lower_ref, lower_far_ref)):
        rows = slice(start, start + HALF)
        total = before_ref[rows] + dot(piece[...], near) + dot(piece_far[...], far)
        out_ref[rows] = total.astype(jnp.bfloat16)


def finish(upper, lower, upper_far, lower_far, weight, before):
    return pl.pallas_call(
        finish_kernel,
        out_shape=jax.ShapeDtypeStruct((BLOCK, BLOCK), jnp.bfloat16),
        in_specs=[whole()] * 6,
        out_specs=whole(),
        compiler_params=params(16),
        name="finish",
    )(upper, lower, upper_far, lower_far, weight, before)


def along(steps):
    return [(i, (i + steps) % 4) for i in range(4)]


def on_device(query, key, value, taps, gain, weight):
    blocks = prepare(key, value, taps)
    got = lax.all_to_all(blocks, TOKENS, 0, 0, tiled=True)
    weight, _ = lax.optimization_barrier((weight, blocks))
    weight = [weight] + [lax.ppermute(weight, "zh", along(k)) for k in (1, 2, 3)]
    conv = convolve(got, gain.reshape(1, BLOCK))
    conv, *weight = lax.optimization_barrier((conv, *weight))
    weight = jnp.stack(weight)
    weight = [weight] + [lax.ppermute(weight, "x", along(k)) for k in (1, 2, 3)]
    conv = lax.all_to_all(conv, TOKENS, 0, 0, tiled=True)
    gated, top, low = gate(conv, query)
    far_top = lax.ppermute(top, "zl", PAIR)
    after = lax.ppermute(gated, "y", along(1))
    ahead = lax.ppermute(gated, "y", along(3))
    far_low = lax.ppermute(low, "zl", PAIR)
    *weight, _, _, _ = lax.optimization_barrier((*weight, after, ahead, far_low))
    weight = jnp.stack(weight)
    weights = order(weight, lax.ppermute(weight, "core", PAIR))
    after_far = [lax.ppermute(part, "y", along(1)) for part in (far_top, far_low)]
    ahead_far = [lax.ppermute(part, "y", along(3)) for part in (far_top, far_low)]
    upper = lax.ppermute(after[:HALF], "y", along(1))
    lower = lax.ppermute(ahead[HALF:], "y", along(3))
    upper_far = lax.ppermute(after_far[0], "y", along(1))
    lower_far = lax.ppermute(ahead_far[1], "y", along(3))
    total = project(
        (0, 0, 0, 1), [gated, after, ahead, far_top, far_low], [weights[0], weights[1], weights[3], weights[0]]
    )
    total = project((1, 1), after_far + ahead_far, [weights[1], weights[3]], total)
    return finish(upper, lower, upper_far, lower_far, weights[2], total)


def solution(mesh):
    fine = Mesh(mesh.devices.reshape(4, 4, 2, 4, 2), AXES)
    columns = ("y", "zl")
    placed = P(TOKENS, columns)
    return jax.shard_map(
        on_device,
        mesh=fine,
        in_specs=(placed, placed, placed, placed, P(columns), placed),
        out_specs=placed,
        check_vma=False,
    )
```

```python
import functools
import math

import jax
import jax.numpy as jnp
import numpy as np
from jax import lax
from jax.experimental import pallas as pl
from jax.experimental.pallas import tpu as pltpu
from jax.sharding import Mesh
from jax.sharding import PartitionSpec as P

AXES = ("x", "zh", "core", "y", "zl")
TOKENS = ("x", "zh", "core")
BLOCKS = 32
BLOCK = 512
CHANNELS = 16
SLICE = 8
HALF = 256
STEPS = 64
INNER = 256
PERIOD = 32768
PAIR = [(0, 1), (1, 0)]


def halves(table):
    high = table.astype(np.float32).astype(jnp.bfloat16)
    low = (table - high.astype(np.float64)).astype(np.float32).astype(jnp.bfloat16)
    return high, low


def tables():
    odd = np.arange(STEPS // 2) + 0.5
    same = np.eye(SLICE)
    first, last = [], []
    for parity in range(2):
        outer = 2 * math.pi * np.outer(odd, 2 * np.arange(BLOCKS) + parity) / (2 * STEPS)
        first.append(np.concatenate([np.kron(np.cos(outer), same), np.kron(-np.sin(outer), same)], 0))
        last.append(first[-1].T / (PERIOD // 2))
    inner = np.arange(INNER)
    turn = 2 * math.pi * np.outer(np.concatenate([odd, STEPS - odd]), inner) / PERIOD
    turn = np.stack([np.cos(turn), np.sin(turn)]).astype(np.float32)
    angle = 2 * math.pi * (np.outer(inner, inner) % INNER) / INNER
    cos_i, sin_i = np.cos(angle), np.sin(angle)
    ahead = np.block([[cos_i, -sin_i], [sin_i, cos_i]])
    back = np.block([[cos_i, sin_i], [-sin_i, cos_i]])
    return (
        np.stack([np.concatenate(halves(table), 1) for table in first]),
        turn,
        np.concatenate(halves(ahead), 0),
        np.concatenate(halves(back), 0),
        np.stack([np.concatenate(halves(table), 1) for table in last]),
    )


def dot(left, right):
    return jnp.dot(left, right, preferred_element_type=jnp.float32)


def split(value):
    high = value.astype(jnp.bfloat16)
    return high, (value - high.astype(jnp.float32)).astype(jnp.bfloat16)


def params(mebibytes):
    return pltpu.CompilerParams(vmem_limit_bytes=mebibytes * 1024 * 1024)


def whole():
    return pl.BlockSpec(memory_space=pltpu.VMEM)


def anywhere():
    return pl.BlockSpec(memory_space=pl.ANY)


def prepare_kernel(key_hbm, value_hbm, filter_hbm, out_hbm, key_ref, value_ref, filter_ref, out_ref, sems, out_sems):
    moves = []
    for i in range(4):
        columns = pl.ds(i * 128, 128)
        for j, (far, near) in enumerate(((key_hbm, key_ref), (value_hbm, value_ref), (filter_hbm, filter_ref))):
            moves.append(pltpu.make_async_copy(far.at[:, columns], near.at[i], sems.at[i, j]))
            moves[-1].start()
    outs = []
    for i in range(4):
        for move in moves[3 * i : 3 * i + 3]:
            move.wait()
        source = key_ref[i].astype(jnp.float32) * value_ref[i].astype(jnp.float32)
        source = source.T.reshape(8, CHANNELS, BLOCK)
        taps = filter_ref[i].T.reshape(8, CHANNELS, BLOCK)
        out_ref[i] = jnp.concatenate([source, taps], 1).astype(jnp.bfloat16)
        outs.append(pltpu.make_async_copy(out_ref.at[i], out_hbm.at[pl.ds(i * 8, 8)], out_sems.at[i]))
        outs[-1].start()
    for out in outs:
        out.wait()


def prepare(key, value, taps):
    return pl.pallas_call(
        prepare_kernel,
        out_shape=jax.ShapeDtypeStruct((BLOCKS, 2 * CHANNELS, BLOCK), jnp.bfloat16),
        in_specs=[anywhere()] * 3,
        out_specs=anywhere(),
        scratch_shapes=[
            pltpu.VMEM((4, BLOCK, 128), jnp.bfloat16),
            pltpu.VMEM((4, BLOCK, 128), jnp.bfloat16),
            pltpu.VMEM((4, BLOCK, 128), jnp.float32),
            pltpu.VMEM((4, 8, 2 * CHANNELS, BLOCK), jnp.bfloat16),
            pltpu.SemaphoreType.DMA((4, 3)),
            pltpu.SemaphoreType.DMA((4,)),
        ],
        compiler_params=params(56),
        name="prepare",
    )(key, value, taps)


def thrice(table_ref):
    return jnp.concatenate([table_ref[:BLOCK], table_ref[...]], 0)


def convolve_kernel(got_ref, gain_ref, turn_ref, *refs):
    out_ref, tables_here, sems = refs[4], refs[5:9], refs[9]
    moves = []
    for i in range(4):
        part = refs[i].shape[-2] // 2
        for j in range(4):
            rows = pl.ds(j % 2 * part, part)
            place = (j // 2, rows) if i in (0, 3) else pl.ds(j * (part // 2), part // 2)
            moves.append(pltpu.make_async_copy(refs[i].at[place], tables_here[i].at[place], sems.at[i, j]))

    def started(i):
        for move in moves[4 * i : 4 * i + 4]:
            move.start()

    def arrived(i):
        for move in moves[4 * i : 4 * i + 4]:
            move.wait()

    started(0)
    first_ref, ahead_ref, back_ref, last_ref = tables_here
    place = lax.axis_index("x") * 8 + lax.axis_index("zh") * 2 + lax.axis_index("core")
    cos_t = turn_ref[0][:, None, :]
    sin_t = turn_ref[1][:, None, :]
    rows = STEPS * SLICE
    half = rows // 2

    def turned(real, imag, sign):
        real = real.reshape(STEPS, SLICE, INNER)
        imag = imag.reshape(STEPS, SLICE, INNER)
        one = real * cos_t - (sign * imag) * sin_t
        two = imag * cos_t + (sign * real) * sin_t
        return one.reshape(rows, INNER), two.reshape(rows, INNER)

    got = got_ref[...].astype(jnp.float32).reshape(BLOCKS, 2, 2, SLICE, BLOCK)
    outs = []
    for s in range(2):
        source = got[:, 0, s].reshape(BLOCKS * SLICE, BLOCK)
        taps = got[:, 1, s].reshape(BLOCKS * SLICE, BLOCK)
        sums = []
        for parity in range(2):
            lanes = slice(parity * INNER, (parity + 1) * INNER)
            both = jnp.concatenate([source[:, lanes], taps[:, lanes]], 1).astype(jnp.bfloat16)
            if s == 0 and parity == 0:
                arrived(0)
                for i in (1, 2, 3):
                    started(i)
            sums.append(dot(first_ref[parity], jnp.concatenate([both, both], 0)))
        even, uneven = sums
        real = jnp.concatenate([even[:half] + uneven[:half], even[:half] - uneven[:half]], 0)
        imag = jnp.concatenate([even[half:] + uneven[half:], uneven[half:] - even[half:]], 0)
        if s == 0:
            arrived(1)
        spectra = []
        for part in range(2):
            columns = slice(part * INNER, (part + 1) * INNER)
            high, low = split(jnp.concatenate(turned(real[:, columns], imag[:, columns], -1.0), 1))
            spectra.append(dot(jnp.concatenate([high, low, high], 1), thrice(ahead_ref)))
        (ar, ai), (br, bi) = [(z[:, :INNER], z[:, INNER:]) for z in spectra]
        product = jnp.concatenate([ar * br - ai * bi, ar * bi + ai * br], 1)
        high, low = split(product)
        if s == 0:
            arrived(2)
        inner = dot(jnp.concatenate([high, low, high], 1), thrice(back_ref))
        real, imag = turned(inner[:, :INNER], inner[:, INNER:], 1.0)
        if s == 0:
            arrived(3)
        conv = []
        for parity, sign in ((0, 1.0), (1, -1.0)):
            real_p = real[:half] + sign * real[half:]
            imag_p = imag[:half] - sign * imag[half:]
            high, low = split(jnp.concatenate([real_p, imag_p], 0))
            table = jnp.concatenate([last_ref[parity, :, :BLOCK], last_ref[parity]], 1)
            conv.append(dot(table, jnp.concatenate([high, low, high], 0)))
        conv = jnp.concatenate(conv, 1)
        channel = place * CHANNELS + s * SLICE + lax.broadcasted_iota(jnp.int32, (SLICE, BLOCK), 0)
        picked = channel == lax.broadcasted_iota(jnp.int32, (SLICE, BLOCK), 1)
        gain = jnp.sum(jnp.where(picked, gain_ref[...], 0.0), 1, keepdims=True)
        outs.append(conv.reshape(BLOCKS, SLICE, BLOCK) + gain[None] * source.reshape(BLOCKS, SLICE, BLOCK))
    out_ref[...] = jnp.concatenate(outs, 1).astype(jnp.bfloat16)


def convolve(got, gain):
    first, turn, ahead, back, last = tables()
    return pl.pallas_call(
        convolve_kernel,
        out_shape=jax.ShapeDtypeStruct((BLOCKS, CHANNELS, BLOCK), jnp.bfloat16),
        in_specs=[whole()] * 3 + [anywhere()] * 4,
        out_specs=whole(),
        scratch_shapes=[pltpu.VMEM(table.shape, jnp.bfloat16) for table in (first, ahead, back, last)]
        + [pltpu.SemaphoreType.DMA((4, 4))],
        compiler_params=params(40),
        name="convolve",
    )(got, gain, turn, first, ahead, back, last)


def gate_kernel(conv_ref, query_ref, out_ref):
    conv = conv_ref[...].astype(jnp.float32).reshape(BLOCK, BLOCK).T
    out_ref[...] = (query_ref[...].astype(jnp.float32) * conv).astype(jnp.bfloat16)


def gate(conv, query):
    return pl.pallas_call(
        gate_kernel,
        out_shape=jax.ShapeDtypeStruct((BLOCK, BLOCK), jnp.bfloat16),
        in_specs=[whole()] * 2,
        out_specs=whole(),
        compiler_params=params(16),
        name="gate",
    )(conv, query)


def project_kernel(items, extras, begins, own_w, sibling_w, *refs):
    pieces, refs = refs[: len(items)], refs[len(items) :]
    before_ref, refs = (None, refs) if begins else (refs[0], refs[1:])
    total_ref, (held, sems) = refs[0], refs[-2:]
    core, x, y, zh, line = (lax.axis_index(axis) for axis in ("core", "x", "y", "zh", "zl"))
    moves = []
    for index, (back, far) in enumerate(items + extras):
        away = lax.rem(x - y + back + 4, 4)
        column = 1 - line if far else line
        out = refs[1].at[index - len(items)] if index >= len(items) else held.at[index]
        for j in range(2):
            k = lax.rem(zh + 4 - 2 * column - j, 4)
            mine, other = pl.ds((2 * j + core) * 128, 128), pl.ds((2 * j + 1 - core) * 128, 128)
            moves.append(pltpu.make_async_copy(own_w.at[away, k], out.at[mine], sems.at[index, j, 0]))
            moves.append(pltpu.make_async_copy(sibling_w.at[away, k], out.at[other], sems.at[index, j, 1]))
    for move in moves:
        move.start()
    total = None if begins else before_ref[...]
    for index, piece in enumerate(pieces):
        for move in moves[4 * index : 4 * index + 4]:
            move.wait()
        term = dot(piece[...], held[index])
        total = term if total is None else total + term
    total_ref[...] = total
    for move in moves[4 * len(items) :]:
        move.wait()


def project(weights, items, pieces, before=None, extras=()):
    count = len(items)
    outs = [jax.ShapeDtypeStruct((BLOCK, BLOCK), jnp.float32)]
    if extras:
        outs.append(jax.ShapeDtypeStruct((len(extras), BLOCK, BLOCK), jnp.bfloat16))
    operands = list(pieces) + ([] if before is None else [before])
    return pl.pallas_call(
        functools.partial(project_kernel, items, extras, before is None),
        out_shape=outs,
        in_specs=[anywhere()] * 2 + [whole()] * len(operands),
        out_specs=[whole()] * len(outs),
        scratch_shapes=[
            pltpu.VMEM((count, BLOCK, BLOCK), jnp.bfloat16),
            pltpu.SemaphoreType.DMA((count + len(extras), 2, 2)),
        ],
        compiler_params=params(16),
        cost_estimate=pl.CostEstimate(
            flops=2 * count * BLOCK**3, bytes_accessed=(count + 3) * 2**20, transcendentals=0
        ),
        name="project",
    )(*weights, *operands)


def finish_kernel(after_ref, ahead_ref, weight_ref, before_ref, out_ref):
    total = before_ref[...] + dot(after_ref[...], weight_ref[0]) + dot(ahead_ref[...], weight_ref[1])
    out_ref[...] = total.astype(jnp.bfloat16)


def finish(after, ahead, weight, before):
    return pl.pallas_call(
        finish_kernel,
        out_shape=jax.ShapeDtypeStruct((BLOCK, BLOCK), jnp.bfloat16),
        in_specs=[whole()] * 4,
        out_specs=whole(),
        compiler_params=params(16),
        name="finish",
    )(after, ahead, weight, before)


def along(steps):
    return [(i, (i + steps) % 4) for i in range(4)]


def on_device(query, key, value, taps, gain, weight):
    blocks = prepare(key, value, taps)
    got = lax.all_to_all(blocks, TOKENS, 0, 0, tiled=True)
    weight, _ = lax.optimization_barrier((weight, blocks))
    weight = [weight] + [lax.ppermute(weight, "zh", along(k)) for k in (1, 2, 3)]
    conv = convolve(got, gain.reshape(1, BLOCK))
    conv, *weight = lax.optimization_barrier((conv, *weight))
    weight = jnp.stack(weight)
    weight = [weight] + [lax.ppermute(weight, "x", along(k)) for k in (1, 2, 3)]
    conv = lax.all_to_all(conv, TOKENS, 0, 0, tiled=True)
    gated = gate(conv, query)
    across = lax.ppermute(gated, "y", along(2))
    far = lax.ppermute(gated, "zl", PAIR)
    after = lax.ppermute(gated, "y", along(1))
    ahead = lax.ppermute(gated, "y", along(3))
    across_far = lax.ppermute(across, "zl", PAIR)
    after_far = lax.ppermute(far, "y", along(1))
    ahead_far = lax.ppermute(far, "y", along(3))
    *weight, _, _ = lax.optimization_barrier((*weight, far, across))
    weight = jnp.stack(weight)
    weight = (weight, lax.ppermute(weight, "core", PAIR))
    (total,) = project(weight, ((0, 0), (0, 1), (2, 0)), [gated, far, across])
    total, last = project(
        weight, ((1, 0), (3, 0), (2, 1)), [after, ahead, across_far], total, ((1, 1), (3, 1))
    )
    return finish(after_far, ahead_far, last, total)


def solution(mesh):
    fine = Mesh(mesh.devices.reshape(4, 4, 2, 4, 2), AXES)
    columns = ("y", "zl")
    placed = P(TOKENS, columns)
    return jax.shard_map(
        on_device,
        mesh=fine,
        in_specs=(placed, placed, placed, placed, P(columns), placed),
        out_specs=placed,
        check_vma=False,
    )
```

```python
import functools
import math

import jax
import jax.numpy as jnp
import numpy as np
from jax import lax
from jax.experimental import pallas as pl
from jax.experimental.pallas import tpu as pltpu
from jax.sharding import Mesh
from jax.sharding import PartitionSpec as P

AXES = ("x", "zh", "core", "y", "zl")
TOKENS = ("x", "zh", "core")
BLOCKS = 32
BLOCK = 512
CHANNELS = 16
SLICE = 8
HALF = 256
STEPS = 64
INNER = 256
PERIOD = 32768
PAIR = [(0, 1), (1, 0)]


def halves(table):
    high = table.astype(np.float32).astype(jnp.bfloat16)
    low = (table - high.astype(np.float64)).astype(np.float32).astype(jnp.bfloat16)
    return high, low


def tables():
    odd = np.arange(STEPS // 2) + 0.5
    same = np.eye(SLICE)
    first, last = [], []
    for parity in range(2):
        outer = 2 * math.pi * np.outer(odd, 2 * np.arange(BLOCKS) + parity) / (2 * STEPS)
        first.append(np.concatenate([np.kron(np.cos(outer), same), np.kron(-np.sin(outer), same)], 0))
        last.append(first[-1].T / (PERIOD // 2))
    inner = np.arange(INNER)
    turn = 2 * math.pi * np.outer(np.concatenate([odd, STEPS - odd]), inner) / PERIOD
    turn = np.stack([np.cos(turn), np.sin(turn)]).astype(np.float32)
    angle = 2 * math.pi * (np.outer(inner, inner) % INNER) / INNER
    cos_i, sin_i = np.cos(angle), np.sin(angle)
    ahead = np.block([[cos_i, -sin_i], [sin_i, cos_i]])
    back = np.block([[cos_i, sin_i], [-sin_i, cos_i]])
    return (
        np.stack([np.concatenate(halves(table), 1) for table in first]),
        turn,
        np.concatenate(halves(ahead), 0),
        np.concatenate(halves(back), 0),
        np.stack([np.concatenate(halves(table), 1) for table in last]),
    )


def dot(left, right):
    return jnp.dot(left, right, preferred_element_type=jnp.float32)


def split(value):
    high = value.astype(jnp.bfloat16)
    return high, (value - high.astype(jnp.float32)).astype(jnp.bfloat16)


def params(mebibytes):
    return pltpu.CompilerParams(vmem_limit_bytes=mebibytes * 1024 * 1024)


def whole():
    return pl.BlockSpec(memory_space=pltpu.VMEM)


def anywhere():
    return pl.BlockSpec(memory_space=pl.ANY)


def prepare_kernel(key_hbm, value_hbm, filter_hbm, out_hbm, key_ref, value_ref, filter_ref, out_ref, sems, out_sems):
    moves = []
    for i in range(4):
        columns = pl.ds(i * 128, 128)
        for j, (far, near) in enumerate(((key_hbm, key_ref), (value_hbm, value_ref), (filter_hbm, filter_ref))):
            moves.append(pltpu.make_async_copy(far.at[:, columns], near.at[i], sems.at[i, j]))
            moves[-1].start()
    outs = []
    for i in range(4):
        for move in moves[3 * i : 3 * i + 3]:
            move.wait()
        source = key_ref[i].astype(jnp.float32) * value_ref[i].astype(jnp.float32)
        source = source.T.reshape(8, CHANNELS, BLOCK)
        taps = filter_ref[i].T.reshape(8, CHANNELS, BLOCK)
        out_ref[i] = jnp.concatenate([source, taps], 1).astype(jnp.bfloat16)
        outs.append(pltpu.make_async_copy(out_ref.at[i], out_hbm.at[pl.ds(i * 8, 8)], out_sems.at[i]))
        outs[-1].start()
    for out in outs:
        out.wait()


def prepare(key, value, taps):
    return pl.pallas_call(
        prepare_kernel,
        out_shape=jax.ShapeDtypeStruct((BLOCKS, 2 * CHANNELS, BLOCK), jnp.bfloat16),
        in_specs=[anywhere()] * 3,
        out_specs=anywhere(),
        scratch_shapes=[
            pltpu.VMEM((4, BLOCK, 128), jnp.bfloat16),
            pltpu.VMEM((4, BLOCK, 128), jnp.bfloat16),
            pltpu.VMEM((4, BLOCK, 128), jnp.float32),
            pltpu.VMEM((4, 8, 2 * CHANNELS, BLOCK), jnp.bfloat16),
            pltpu.SemaphoreType.DMA((4, 3)),
            pltpu.SemaphoreType.DMA((4,)),
        ],
        compiler_params=params(56),
        name="prepare",
    )(key, value, taps)


def thrice(table_ref):
    return jnp.concatenate([table_ref[:BLOCK], table_ref[...]], 0)


def convolve_kernel(got_ref, gain_ref, turn_ref, *refs):
    out_ref, tables_here, sems = refs[4], refs[5:9], refs[9]
    moves = []
    for i in range(4):
        part = refs[i].shape[-2] // 2
        for j in range(4):
            rows = pl.ds(j % 2 * part, part)
            place = (j // 2, rows) if i in (0, 3) else pl.ds(j * (part // 2), part // 2)
            moves.append(pltpu.make_async_copy(refs[i].at[place], tables_here[i].at[place], sems.at[i, j]))

    def started(i):
        for move in moves[4 * i : 4 * i + 4]:
            move.start()

    def arrived(i):
        for move in moves[4 * i : 4 * i + 4]:
            move.wait()

    started(0)
    first_ref, ahead_ref, back_ref, last_ref = tables_here
    place = lax.axis_index("x") * 8 + lax.axis_index("zh") * 2 + lax.axis_index("core")
    cos_t = turn_ref[0][:, None, :]
    sin_t = turn_ref[1][:, None, :]
    rows = STEPS * SLICE
    half = rows // 2

    def turned(real, imag, sign):
        real = real.reshape(STEPS, SLICE, INNER)
        imag = imag.reshape(STEPS, SLICE, INNER)
        one = real * cos_t - (sign * imag) * sin_t
        two = imag * cos_t + (sign * real) * sin_t
        return one.reshape(rows, INNER), two.reshape(rows, INNER)

    got = got_ref[...].astype(jnp.float32).reshape(BLOCKS, 2, 2, SLICE, BLOCK)
    outs = []
    for s in range(2):
        source = got[:, 0, s].reshape(BLOCKS * SLICE, BLOCK)
        taps = got[:, 1, s].reshape(BLOCKS * SLICE, BLOCK)
        sums = []
        for parity in range(2):
            lanes = slice(parity * INNER, (parity + 1) * INNER)
            both = jnp.concatenate([source[:, lanes], taps[:, lanes]], 1).astype(jnp.bfloat16)
            if s == 0 and parity == 0:
                arrived(0)
                for i in (1, 2, 3):
                    started(i)
            sums.append(dot(first_ref[parity], jnp.concatenate([both, both], 0)))
        even, uneven = sums
        real = jnp.concatenate([even[:half] + uneven[:half], even[:half] - uneven[:half]], 0)
        imag = jnp.concatenate([even[half:] + uneven[half:], uneven[half:] - even[half:]], 0)
        if s == 0:
            arrived(1)
        spectra = []
        for part in range(2):
            columns = slice(part * INNER, (part + 1) * INNER)
            high, low = split(jnp.concatenate(turned(real[:, columns], imag[:, columns], -1.0), 1))
            spectra.append(dot(jnp.concatenate([high, low, high], 1), thrice(ahead_ref)))
        (ar, ai), (br, bi) = [(z[:, :INNER], z[:, INNER:]) for z in spectra]
        product = jnp.concatenate([ar * br - ai * bi, ar * bi + ai * br], 1)
        high, low = split(product)
        if s == 0:
            arrived(2)
        inner = dot(jnp.concatenate([high, low, high], 1), thrice(back_ref))
        real, imag = turned(inner[:, :INNER], inner[:, INNER:], 1.0)
        if s == 0:
            arrived(3)
        conv = []
        for parity, sign in ((0, 1.0), (1, -1.0)):
            real_p = real[:half] + sign * real[half:]
            imag_p = imag[:half] - sign * imag[half:]
            high, low = split(jnp.concatenate([real_p, imag_p], 0))
            table = jnp.concatenate([last_ref[parity, :, :BLOCK], last_ref[parity]], 1)
            conv.append(dot(table, jnp.concatenate([high, low, high], 0)))
        conv = jnp.concatenate(conv, 1)
        channel = place * CHANNELS + s * SLICE + lax.broadcasted_iota(jnp.int32, (SLICE, BLOCK), 0)
        picked = channel == lax.broadcasted_iota(jnp.int32, (SLICE, BLOCK), 1)
        gain = jnp.sum(jnp.where(picked, gain_ref[...], 0.0), 1, keepdims=True)
        outs.append(conv.reshape(BLOCKS, SLICE, BLOCK) + gain[None] * source.reshape(BLOCKS, SLICE, BLOCK))
    out_ref[...] = jnp.concatenate(outs, 1).astype(jnp.bfloat16)


def convolve(got, gain):
    first, turn, ahead, back, last = tables()
    return pl.pallas_call(
        convolve_kernel,
        out_shape=jax.ShapeDtypeStruct((BLOCKS, CHANNELS, BLOCK), jnp.bfloat16),
        in_specs=[whole()] * 3 + [anywhere()] * 4,
        out_specs=whole(),
        scratch_shapes=[pltpu.VMEM(table.shape, jnp.bfloat16) for table in (first, ahead, back, last)]
        + [pltpu.SemaphoreType.DMA((4, 4))],
        compiler_params=params(40),
        name="convolve",
    )(got, gain, turn, first, ahead, back, last)


def gate_kernel(conv_ref, query_ref, out_ref):
    conv = conv_ref[...].astype(jnp.float32).reshape(BLOCK, BLOCK).T
    out_ref[...] = (query_ref[...].astype(jnp.float32) * conv).astype(jnp.bfloat16)


def gate(conv, query):
    return pl.pallas_call(
        gate_kernel,
        out_shape=jax.ShapeDtypeStruct((BLOCK, BLOCK), jnp.bfloat16),
        in_specs=[whole()] * 2,
        out_specs=whole(),
        compiler_params=params(16),
        name="gate",
    )(conv, query)


def project_kernel(items, extras, begins, own_w, sibling_w, *refs):
    pieces, refs = refs[: len(items)], refs[len(items) :]
    before_ref, refs = (None, refs) if begins else (refs[0], refs[1:])
    total_ref, (held, sems) = refs[0], refs[-2:]
    core, x, y, zh, line = (lax.axis_index(axis) for axis in ("core", "x", "y", "zh", "zl"))
    moves = []
    for index, (back, far) in enumerate(items + extras):
        away = lax.rem(x - y + back + 4, 4)
        column = 1 - line if far else line
        out = refs[1].at[index - len(items)] if index >= len(items) else held.at[index]
        for j in range(2):
            k = lax.rem(zh + 4 - 2 * column - j, 4)
            mine, other = pl.ds((2 * j + core) * 128, 128), pl.ds((2 * j + 1 - core) * 128, 128)
            moves.append(pltpu.make_async_copy(own_w.at[away, k], out.at[mine], sems.at[index, j, 0]))
            moves.append(pltpu.make_async_copy(sibling_w.at[away, k], out.at[other], sems.at[index, j, 1]))
    for move in moves:
        move.start()
    total = None if begins else before_ref[...]
    for index, piece in enumerate(pieces):
        for move in moves[4 * index : 4 * index + 4]:
            move.wait()
        term = dot(piece[...], held[index])
        total = term if total is None else total + term
    total_ref[...] = total
    for move in moves[4 * len(items) :]:
        move.wait()


def project(weights, items, pieces, before=None, extras=()):
    count = len(items)
    outs = [jax.ShapeDtypeStruct((BLOCK, BLOCK), jnp.float32)]
    if extras:
        outs.append(jax.ShapeDtypeStruct((len(extras), BLOCK, BLOCK), jnp.bfloat16))
    operands = list(pieces) + ([] if before is None else [before])
    return pl.pallas_call(
        functools.partial(project_kernel, items, extras, before is None),
        out_shape=outs,
        in_specs=[anywhere()] * 2 + [whole()] * len(operands),
        out_specs=[whole()] * len(outs),
        scratch_shapes=[
            pltpu.VMEM((count, BLOCK, BLOCK), jnp.bfloat16),
            pltpu.SemaphoreType.DMA((count + len(extras), 2, 2)),
        ],
        compiler_params=params(16),
        cost_estimate=pl.CostEstimate(
            flops=2 * count * BLOCK**3, bytes_accessed=(count + 3) * 2**20, transcendentals=0
        ),
        name="project",
    )(*weights, *operands)


def finish_kernel(after_ref, ahead_ref, weight_ref, before_ref, out_ref):
    total = before_ref[...] + dot(after_ref[...], weight_ref[0]) + dot(ahead_ref[...], weight_ref[1])
    out_ref[...] = total.astype(jnp.bfloat16)


def finish(after, ahead, weight, before):
    return pl.pallas_call(
        finish_kernel,
        out_shape=jax.ShapeDtypeStruct((BLOCK, BLOCK), jnp.bfloat16),
        in_specs=[whole()] * 4,
        out_specs=whole(),
        compiler_params=params(16),
        name="finish",
    )(after, ahead, weight, before)


def along(steps):
    return [(i, (i + steps) % 4) for i in range(4)]


def on_device(query, key, value, taps, gain, weight):
    blocks = prepare(key, value, taps)
    got = lax.all_to_all(blocks, TOKENS, 0, 0, tiled=True)
    weight, _ = lax.optimization_barrier((weight, blocks))
    next_1, next_3 = [lax.ppermute(weight, "zh", along(k)) for k in (1, 3)]
    next_top = lax.ppermute(next_1[:64], "zh", along(1))
    next_low = lax.ppermute(next_3[64:], "zh", along(3))
    weight = [weight, next_1, next_top, next_low, next_3]
    conv = convolve(got, gain.reshape(1, BLOCK))
    conv, *weight = lax.optimization_barrier((conv, *weight))
    weight = jnp.concatenate(weight, 0).reshape(4, 128, BLOCK)
    weight_1, weight_3 = [lax.ppermute(weight, "x", along(k)) for k in (1, 3)]
    weight_top = lax.ppermute(weight_1[:2], "x", along(1))
    weight_low = lax.ppermute(weight_3[2:], "x", along(3))
    weight = [weight, weight_1, weight_top, weight_low, weight_3]
    conv = lax.all_to_all(conv, TOKENS, 0, 0, tiled=True)
    gated = gate(conv, query)
    across = lax.ppermute(gated, "y", along(2))
    far = lax.ppermute(gated, "zl", PAIR)
    after = lax.ppermute(gated, "y", along(1))
    ahead = lax.ppermute(gated, "y", along(3))
    across_far = lax.ppermute(across, "zl", PAIR)
    after_far = lax.ppermute(far, "y", along(1))
    ahead_far = lax.ppermute(far, "y", along(3))
    *weight, _, _ = lax.optimization_barrier((*weight, far, across))
    weight = jnp.concatenate(weight, 0).reshape(4, 4, 128, BLOCK)
    weight = (weight, lax.ppermute(weight, "core", PAIR))
    (total,) = project(weight, ((0, 0), (0, 1), (2, 0)), [gated, far, across])
    total, last = project(
        weight, ((1, 0), (3, 0), (2, 1)), [after, ahead, across_far], total, ((1, 1), (3, 1))
    )
    return finish(after_far, ahead_far, last, total)


def solution(mesh):
    fine = Mesh(mesh.devices.reshape(4, 4, 2, 4, 2), AXES)
    columns = ("y", "zl")
    placed = P(TOKENS, columns)
    return jax.shard_map(
        on_device,
        mesh=fine,
        in_specs=(placed, placed, placed, placed, P(columns), placed),
        out_specs=placed,
        check_vma=False,
    )
```
